256 devices in a mesh: row: 8 (over z_lo, x), col: 32 (over z_hi, y, core).
Axes of the slice: x: 4, y: 4, z: 8 (z_hi: 4, z_lo: 2; z = z_hi * 2 + z_lo), core: 2. Of those that a mesh axis runs over, the one named last changes fastest.
Arguments:
- embeddings: bfloat16 [32768, 1536], P(('row', 'col')), may hold values from -6 to 6
- membership: int32 [32768, 1], P(('row', 'col')), may hold values from 0 to 7; in each aligned block of 128 rows (0 to 127, 128 to 255, ...) at most 24 rows name the same one
- selected: int32 [8, 8], replicated, may hold values from 0 to 32767
Outputs:
- gains: float32 [32768], P(('row', 'col'))
The draws below stay inside these ranges and needn't reach their ends.
Inputs may be any that keep to these rules, and one draw needn't show every extreme that they name: `membership`: among the 128 images of one device (aligned blocks in order), at most 24 belong to one window; some window reaches 24 images.
All inputs are finite; a program needn't handle non-finite values.
Results may differ from the reference program's by a relative error of at most 0.0003.
Values may be sent and summed in bfloat16 or wider, within the bound.
A program may use at most 64 MiB of HBM per device.

```python
import math
import jax
import jax.numpy as jnp
import numpy as np
from jax import lax

D = 1536
ROWS_DEV = 128
PICKS = 8
WINDOWS = 8
CAP = 24
NPTS = 32768


def touch_ends(result, stream_key, least, largest):
    longest = result.shape.index(max(result.shape))
    spots = []
    for shift in (0, 1):
        where = [jax.random.randint(jax.random.fold_in(stream_key, axis), (), 0, length) for axis, length in enumerate(result.shape)]
        where[longest] = (where[longest] + shift) % result.shape[longest]
        spots.append(tuple(where))
    return result.at[spots[0]].set(least).at[spots[1]].set(largest)


def block_scale(rng, shape, shards, smallest, high):
    def one(axis_at, shards_of):
        draws = jax.random.uniform(jax.random.fold_in(jax.random.fold_in(rng, 6), axis_at), (shards_of,), jnp.float32, smallest / len(shards), high / len(shards))
        return jnp.repeat(jnp.exp(draws), shape[axis_at] // shards_of).reshape((-1,) + (1,) * (len(shape) - axis_at - 1))

    loudness = one(*shards[0])
    for cut in shards[1:]:
        loudness = loudness * one(*cut)
    return loudness


def deal_out(key, own, number, rows, number_of, top, limit, slope):
    order = jax.random.permutation(key, number_of)
    packed, usual = shares(number_of, rows * top, limit, slope, True), shares(number_of, rows * top, limit, slope, False)
    places = jnp.arange(number_of)

    def named(sizes, turn):
        used = int((sizes > 0).sum())
        fixed = max(1, used // 4)
        moved = fixed + (places - fixed + turn * (used - fixed)) % max(1, number_of - fixed)
        return jnp.zeros((number_of,), jnp.int32).at[order[jnp.where(places < fixed, places, moved)]].set(jnp.asarray(sizes, jnp.int32))

    sizes = jnp.where(number % 4 == 0, named(packed, number // 4), named(usual, number - number // 4 - 1))
    mixed = jax.random.permutation(jax.random.fold_in(own, 3), number_of)
    giver, sink = mixed[0:number_of // 2 * 2:2], mixed[1:number_of // 2 * 2:2]
    margin = jnp.minimum(sizes[giver] - 1, limit - sizes[sink]) // 2
    margin = jnp.where((giver == order[0]) | (sink == order[0]) | (sizes[sink] == 0), 0, jnp.maximum(margin, 0))
    moved = jax.random.randint(jax.random.fold_in(own, 4), (number_of // 2,), 0, 1 << 20) % (margin + 1)
    sizes = sizes.at[giver].add(-moved).at[sink].add(moved)
    labels = jnp.searchsorted(jnp.cumsum(sizes), jnp.arange(rows * top), side="right").astype(jnp.int32)
    grid = labels.reshape(top, rows).T
    grid = grid[jax.random.permutation(jax.random.fold_in(own, 1), rows)]
    turn = jax.random.randint(jax.random.fold_in(own, 2), (rows, 1), 0, top)
    return jnp.take_along_axis(grid, (jnp.arange(top)[None, :] + turn) % top, axis=1)


def shares(number_of, total, bound, lean, full):
    weights = [(1 << 20) // math.isqrt(standing ** lean) + 1 for standing in range(1, number_of + 1)]
    largest = bound if full else min(bound, max(-(-total // number_of), total * weights[0] // sum(weights)))
    least = 1 if total - largest >= number_of - 1 else 0
    holding, surplus = [largest] + [least] * (number_of - 1), total - largest - least * (number_of - 1)
    while surplus > 0:
        movable = [i for i in range(1, number_of) if holding[i] < largest] or [i for i in range(1, number_of) if holding[i] < bound]
        mass, budget = sum([weights[i] for i in movable]), surplus
        for i in movable:
            extra = min(bound - holding[i], max(1, budget * weights[i] // mass), surplus)
            holding[i] = holding[i] + extra
            surplus = surplus - extra
    return np.array(holding)


def noise(key, dims, spread, bound, shards=(), held_as=jnp.bfloat16):
    loudness = block_scale(key, dims, shards, -0.22, 0.18) if shards else 1.0
    array = jax.random.normal(key, dims, jnp.float32) * spread * loudness
    return jnp.minimum(jnp.maximum(array, -bound), bound).astype(held_as)


def setup_inputs(seed: int = 0) -> dict:
    keys = jax.random.split(jax.random.key(seed), 4)
    embeddings = noise(keys[0], (NPTS, D), 1.0, 6.0, ((0, 256),))
    membership_keys = jax.random.split(jax.random.fold_in(keys[1], 1), NPTS // ROWS_DEV)
    membership_turns = jax.random.permutation(jax.random.fold_in(keys[1], 3), NPTS // ROWS_DEV)
    membership = jax.vmap(lambda own, number: deal_out(jax.random.fold_in(keys[1], 2), own, number, ROWS_DEV, WINDOWS, 1, CAP, 0))(membership_keys, membership_turns).reshape((NPTS, 1))
    selected = touch_ends(jax.random.randint(keys[2], (WINDOWS, PICKS), 0, NPTS), jax.random.fold_in(keys[2], 1), 0, NPTS - 1).astype(jnp.int32)
    return dict(embeddings=embeddings, membership=membership, selected=selected)


GAIN_SCALE = 1.0 / 64.0

def reference(embeddings, membership, selected):
    sim_scale = 1.0 / math.sqrt(D)
    member_ids = membership[:, 0]
    chosen = embeddings[selected.reshape(-1)]
    similar = jnp.dot(embeddings, chosen.T, preferred_element_type=jnp.float32) * sim_scale
    best_by_window = lax.optimization_barrier(jnp.max(similar.reshape(NPTS, WINDOWS, PICKS), axis=2))
    in_window = member_ids[:, None] == jnp.arange(WINDOWS, dtype=jnp.int32)[None, :]
    cover_vals = jnp.maximum(lax.optimization_barrier(jnp.sum(jnp.where(in_window, best_by_window, 0.0), axis=1)), 0.0)
    block_rows = math.gcd(NPTS, 512)

    def block_gain(operands):
        cand_block, win_block = operands
        tile_sims = jnp.dot(cand_block, embeddings.T, preferred_element_type=jnp.float32) * sim_scale
        same_win = win_block[:, None] == member_ids[None, :]
        return lax.optimization_barrier(jnp.sum(jnp.where(same_win, jnp.maximum(tile_sims - cover_vals[None, :], 0.0), 0.0), axis=1))
    gain_terms = lax.map(block_gain, (embeddings.reshape(-1, block_rows, D), member_ids.reshape(-1, block_rows)))
    return gain_terms.reshape(-1) * GAIN_SCALE
```

```python
import functools
import math

import jax
import jax.numpy as jnp
from jax import lax
from jax.experimental import pallas as pl
from jax.experimental.pallas import tpu as pltpu
from jax.sharding import PartitionSpec as P

GAIN_SCALE = 1.0 / 64.0
MESH = pl.DeviceIdType.MESH
F32, BF16, I32 = jnp.float32, jnp.bfloat16, jnp.int32

CAP = 24
WIN = 8
PICKS = 8
RING = 4
WAVES = (0, 1, 7, 2, 6, 3, 5, 4)
ZK, XP, XM, X3, YP, YM, Y3, K0 = range(8)


def coords():
    row, col = lax.axis_index("row"), lax.axis_index("col")
    x, z_lo = lax.rem(row, 4), lax.div(row, 4)
    z_hi, y, k = lax.div(col, 8), lax.rem(lax.div(col, 2), 4), lax.rem(col, 2)
    return x, y, z_hi * 2 + z_lo, k


def device(x, y, z, k):
    return lax.rem(z, 2) * 4 + x, lax.div(z, 2) * 8 + y * 2 + k


def rows_dot(left, right):
    return lax.dot_general(left, right, (((1,), (1,)), ((), ())), preferred_element_type=F32)


def kernel(
    emb, mem, sel, out,
    sort, pick, rawx, rawy, raws, s1r, s2s, s2r, s3r, s3s, s4r, chosen,
    points, cands, cov, acc, gs, gy, ts, gz,
    wsend, wrecv, csend, crecv, gsend, grecv,
):
    x, y, z, k = coords()
    rows, width = emb.shape
    half = width // 2
    scale = 1.0 / math.sqrt(width)
    q = x * 2 + k

    def at(dx=0, dy=0, dz=0, dk=0):
        return device(
            lax.rem(x + dx, 4), lax.rem(y + dy, 4), lax.rem(z + dz, 8), lax.rem(k + dk, 2)
        )

    def at_q(d):
        other = lax.rem(q + d, 8)
        return device(lax.div(other, 2), y, z, lax.rem(other, 2))

    def copy(src, dst, ssem, rsem, to):
        return pltpu.make_async_remote_copy(
            src_ref=src, dst_ref=dst, send_sem=ssem, recv_sem=rsem, device_id=to, device_id_type=MESH
        )

    barrier = pltpu.get_barrier_semaphore()
    peers = [at(dz=d) for d in range(1, 8)] + [at_q(d) for d in range(1, 8)] + [at(dy=d) for d in range(1, 4)]
    for peer in peers:
        pl.semaphore_signal(barrier, inc=1, device_id=peer, device_id_type=MESH)

    win = mem[...]
    up = lax.rem(z - win + 8, 8)
    wave = jnp.where(up == 0, 0, jnp.where(up <= 4, 2 * up - 1, 16 - 2 * up))
    in_wave = lax.broadcasted_iota(I32, (WIN, rows), 0) == wave
    before = lax.broadcasted_iota(I32, (rows, rows), 0) < lax.broadcasted_iota(I32, (rows, rows), 1)
    ahead = jnp.dot(
        jnp.where(in_wave, 1.0, 0.0).astype(BF16), jnp.where(before, 1.0, 0.0).astype(BF16),
        preferred_element_type=F32,
    )
    place = jnp.sum(jnp.where(in_wave, ahead, 0.0), axis=0, keepdims=True).astype(I32)
    slot = wave * CAP + place
    slots = WIN * CAP
    sorter = jnp.where(lax.broadcasted_iota(I32, (slots, rows), 0) == slot, 1.0, 0.0)
    base = (lax.axis_index("row") * 32 + lax.axis_index("col")) * rows
    local = base + lax.broadcasted_iota(I32, (PICKS, rows), 1)
    eye = lax.broadcasted_iota(I32, (PICKS, PICKS), 0) == lax.broadcasted_iota(I32, (PICKS, PICKS), 1)
    pickers = []
    for g in range(WIN):
        ids = jnp.sum(jnp.where(eye, sel[g : g + 1, :].astype(F32), 0.0), axis=1, keepdims=True)
        pickers.append(jnp.where(local == ids.astype(I32), 1.0, 0.0))
    onehot = jnp.concatenate([sorter] + pickers, axis=0).astype(BF16)
    low = jnp.dot(onehot, emb[:, :half], preferred_element_type=F32)
    high = jnp.dot(onehot, emb[:, half:], preferred_element_type=F32)
    for g in range(WIN):
        lo, hi = slots + g * PICKS, slots + (g + 1) * PICKS
        pick[g] = jnp.concatenate([low[lo:hi], high[lo:hi]], axis=0).astype(BF16)
    for n in range(WIN):
        lo, hi = n * CAP, (n + 1) * CAP
        part = jnp.concatenate([low[lo:hi], high[lo:hi]], axis=0).astype(BF16)
        if n == 0:
            rawx[0, 0] = part
        else:
            sort[n - 1] = part
    acc[...] = jnp.zeros_like(acc)

    pl.semaphore_wait(barrier, len(peers))

    started = []

    def start(cp):
        cp.start()
        started.append(cp)
        return cp

    picks1 = []
    for d in range(1, 8):
        g = lax.rem(z - lax.rem(q + d, 8) + 8, 8)
        picks1.append(start(copy(pick.at[g], s1r.at[d - 1], csend.at[d - 1], crecv.at[d - 1], at_q(d))))

    def zcopy(n):
        return start(
            copy(sort.at[n - 1], rawx.at[n, 0], wsend.at[n, ZK], wrecv.at[n, ZK], at(dz=8 - WAVES[n]))
        )

    wave_copies = {}

    def wcopy(n, kind, src, dst, to):
        wave_copies[n, kind] = start(copy(src, dst, wsend.at[n, kind], wrecv.at[n, kind], to))

    def level0(n):
        if n > 0:
            zs[n].wait_recv()
        own = rawx.at[n, 0]
        wcopy(n, XP, own, rawx.at[n, 1], at(dx=1))
        wcopy(n, YP, own, rawy.at[n, 0], at(dy=1))
        wcopy(n, XM, own, rawx.at[n, 2], at(dx=3))
        wcopy(n, YM, own, rawy.at[n, 1], at(dy=3))
        wcopy(n, K0, own, raws.at[n, 0], at(dk=1))

    def level1(n):
        first, second = ((XP, YP, 1), (XM, YM, 2)) if n % 2 == 0 else ((XM, YM, 2), (XP, YP, 1))
        xk, yk, s = first
        on = 1 if s == 1 else 3
        wave_copies[n, xk].wait_recv()
        wcopy(n, X3, rawx.at[n, s], rawx.at[n, 3], at(dx=on))
        wcopy(n, K0 + s, rawx.at[n, s], raws.at[n, s], at(dk=1))
        wave_copies[n, yk].wait_recv()
        wcopy(n, Y3, rawy.at[n, s - 1], rawy.at[n, 2], at(dy=on))
        xk, yk, s = second
        wave_copies[n, xk].wait_recv()
        wcopy(n, K0 + s, rawx.at[n, s], raws.at[n, s], at(dk=1))
        wave_copies[n, yk].wait_recv()

    def level2(n):
        wave_copies[n, X3].wait_recv()
        wcopy(n, K0 + 3, rawx.at[n, 3], raws.at[n, 3], at(dk=1))
        wave_copies[n, Y3].wait_recv()

    def level3(n):
        for s in range(RING):
            wave_copies[n, K0 + s].wait_recv()

    def chosen1():
        total = pick[lax.rem(z - q + 8, 8)].astype(F32)
        for d in range(7):
            picks1[d].wait_recv()
            total = total + s1r[d].astype(F32)
        s2s[...] = total.astype(BF16)
        cp = copy(s2s, s2r, csend.at[7], crecv.at[7], at(dz=8 - q))

        @pl.when(q == 0)
        def _():
            s2r[...] = s2s[...]

        @pl.when(q != 0)
        def _():
            cp.start()

        return cp

    def chosen2(cp):
        @pl.when(q != 0)
        def _():
            cp.wait()

        return [
            start(copy(s2r, s3r.at[d - 1], csend.at[7 + d], crecv.at[7 + d], at(dy=d))) for d in range(1, 4)
        ]

    def chosen3(cps):
        total = s2r[...].astype(F32)
        for d in range(3):
            cps[d].wait_recv()
            total = total + s3r[d].astype(F32)
        s3s[...] = total.astype(BF16)
        return [
            start(copy(s3s, s4r.at[d - 1], csend.at[10 + d], crecv.at[10 + d], at_q(d))) for d in range(1, 8)
        ]

    def chosen4(cps):
        total = s3s[...].astype(F32)
        for d in range(7):
            cps[d].wait_recv()
            total = total + s4r[d].astype(F32)
        whole = jnp.concatenate([total[:PICKS], total[PICKS:]], axis=1)
        chosen[...] = jnp.concatenate([whole, whole], axis=0).astype(BF16)

    pair = 2 * CAP
    prow, crow = 2 * RING * pair, RING * pair

    def assemble(group):
        def put(dst, row, ref, s):
            a, b = ref[2 * group, s].astype(F32), ref[2 * group + 1, s].astype(F32)
            dst[row : row + pair, :half] = jnp.concatenate([a[:CAP], b[:CAP]], axis=0).astype(BF16)
            dst[row : row + pair, half:] = jnp.concatenate([a[CAP:], b[CAP:]], axis=0).astype(BF16)

        for s in range(RING):
            put(points, group * prow + s * pair, rawx, s)
            put(points, group * prow + crow + s * pair, raws, s)
            put(cands, group * crow + s * pair, *((rawx, 0) if s == 0 else (rawy, s - 1)))

    def cover(group):
        near = rows_dot(points[group * prow : (group + 1) * prow, :], chosen[...]) * scale
        cov[group * prow : (group + 1) * prow, :] = jnp.maximum(jnp.max(near, axis=1, keepdims=True), 0.0)

    def unit(a, b):
        lo = pl.multiple_of(a * prow, prow)
        sims = rows_dot(points[pl.ds(lo, prow), :], cands[pl.ds(pl.multiple_of(b * crow, crow), crow), :])
        terms = jnp.maximum(sims * scale - cov[pl.ds(lo, prow), :], 0.0)
        acc[b] += jnp.sum(terms.reshape(prow // 8, 8, crow), axis=0)

    def fold(group):
        assemble(group)
        cover(group)

        def body(i, carry):
            a = jnp.where(i <= group, group, i - group - 1)
            b = jnp.where(i <= group, i, group)
            unit(a, b)
            return carry

        lax.fori_loop(0, 2 * group + 1, body, 0)

    zs = {n: zcopy(n) for n in (1, 2, 3, 4)}
    level0(0)
    c2 = chosen1()
    level0(1)
    level1(0)
    zs[5] = zcopy(5)
    level0(2)
    zs[6] = zcopy(6)
    c3 = chosen2(c2)
    level1(1)
    level2(0)
    level0(3)
    zs[7] = zcopy(7)
    level1(2)
    level2(1)
    c4 = chosen3(c3)
    level0(4)
    level1(3)
    level2(2)
    level0(5)
    level1(4)
    level2(3)
    chosen4(c4)
    level3(0)
    level3(1)
    fold(0)
    level0(6)
    level1(5)
    level2(4)
    level3(2)
    level3(3)
    fold(1)
    level0(7)
    level1(6)
    level2(5)
    level1(7)
    level2(6)
    level3(4)
    level3(5)
    fold(2)
    level2(7)
    level3(6)
    level3(7)
    fold(3)

    groups = WIN // 2
    part = jnp.concatenate(
        [jnp.sum(acc[b], axis=0, keepdims=True) for b in range(groups)] + [jnp.zeros((8 - groups, crow), F32)], axis=0
    )
    gs[...] = jnp.concatenate([part, jnp.zeros((8, 256 - crow), F32)], axis=1)
    back = [start(copy(gs, gy.at[i], gsend.at[i], grecv.at[i], at(dy=d))) for i, d in enumerate((1, 3, 2))]
    total = gs[...]
    for i, s in enumerate((2, 1, 3)):
        back[i].wait_recv()
        total = total + pltpu.roll(gy[i], 256 - s * pair, 1)
    ts[...] = total[:, :128]
    home = [
        start(copy(ts, gz.at[n - 1], gsend.at[2 + n], grecv.at[2 + n], at(dz=WAVES[n]))) for n in range(1, 8)
    ]
    row_id = lax.broadcasted_iota(I32, (8, 128), 0)
    lane = lax.broadcasted_iota(I32, (8, 128), 1)
    shift = lax.rem(wave, 2) * CAP + place
    spread = jnp.where(lax.broadcasted_iota(I32, (128, rows), 0) == shift, 1.0, 0.0)
    gathered = jnp.zeros((8, 128), F32)
    for n in range(8):
        if n > 0:
            home[n - 1].wait_recv()
        got = ts[...] if n == 0 else gz[n - 1]
        first = (n % 2) * CAP
        here = (row_id == n // 2) & (lane >= first) & (lane < first + CAP)
        gathered = gathered + jnp.where(here, got, 0.0)
    placed = jnp.dot(gathered, spread, precision=lax.Precision.HIGHEST, preferred_element_type=F32)
    mine = lax.broadcasted_iota(I32, (8, rows), 0) == lax.div(wave, 2)
    out[...] = jnp.sum(jnp.where(mine, placed, 0.0), axis=0, keepdims=True) * GAIN_SCALE
    for cp in started:
        cp.wait_send()


def shards(embeddings, membership, selected):
    rows, width = embeddings.shape
    half = width // 2
    chunk, short = (2 * CAP, half), (2 * PICKS, half)
    dma = pltpu.SemaphoreType.DMA
    vmem = pl.BlockSpec(memory_space=pltpu.VMEM)
    gains = pl.pallas_call(
        kernel,
        out_shape=jax.ShapeDtypeStruct((1, rows), F32),
        in_specs=[vmem] * 3,
        out_specs=vmem,
        scratch_shapes=[
            pltpu.VMEM((7,) + chunk, BF16),
            pltpu.VMEM((8,) + short, BF16),
            pltpu.VMEM((8, 4) + chunk, BF16),
            pltpu.VMEM((8, 3) + chunk, BF16),
            pltpu.VMEM((8, 4) + chunk, BF16),
            pltpu.VMEM((7,) + short, BF16),
            pltpu.VMEM(short, BF16),
            pltpu.VMEM(short, BF16),
            pltpu.VMEM((3,) + short, BF16),
            pltpu.VMEM(short, BF16),
            pltpu.VMEM((7,) + short, BF16),
            pltpu.VMEM((2 * PICKS, width), BF16),
            pltpu.VMEM((8 * 8 * CAP, width), BF16),
            pltpu.VMEM((8 * 4 * CAP, width), BF16),
            pltpu.VMEM((8 * 8 * CAP, 1), F32),
            pltpu.VMEM((4, 8, 8 * CAP), F32),
            pltpu.VMEM((8, 256), F32),
            pltpu.VMEM((3, 8, 256), F32),
            pltpu.VMEM((8, 128), F32),
            pltpu.VMEM((7, 8, 128), F32),
            dma((8, 11)), dma((8, 11)), dma((18,)), dma((18,)), dma((10,)), dma((10,)),
        ],
        compiler_params=pltpu.CompilerParams(
            collective_id=0, has_side_effects=True, vmem_limit_bytes=40 * 1024 * 1024
        ),
    )(embeddings, membership.reshape(1, rows), selected)
    return gains.reshape(rows)


def solution(mesh):
    in_specs = (P(("row", "col"), None), P(("row", "col"), None), P())
    out_specs = P(("row", "col"))
    return jax.shard_map(shards, mesh=mesh, in_specs=in_specs, out_specs=out_specs, check_vma=False)
```

```python
import functools
import math

import jax
import jax.numpy as jnp
from jax import lax
from jax.experimental import pallas as pl
from jax.experimental.pallas import tpu as pltpu
from jax.sharding import PartitionSpec as P

GAIN_SCALE = 1.0 / 64.0
MESH = pl.DeviceIdType.MESH
F32, BF16, I32 = jnp.float32, jnp.bfloat16, jnp.int32

CAP = 24
WIN = 8
PICKS = 8
RING = 4
WAVES = (0, 1, 7, 2, 6, 3, 5, 4)
ZK, XP, XM, X3, YP, YM, Y3, KK = range(8)


def coords():
    row, col = lax.axis_index("row"), lax.axis_index("col")
    x, z_lo = lax.rem(row, 4), lax.div(row, 4)
    z_hi, y, k = lax.div(col, 8), lax.rem(lax.div(col, 2), 4), lax.rem(col, 2)
    return x, y, z_hi * 2 + z_lo, k


def device(x, y, z, k):
    return lax.rem(z, 2) * 4 + x, lax.div(z, 2) * 8 + y * 2 + k


def rows_dot(left, right):
    return lax.dot_general(left, right, (((1,), (1,)), ((), ())), preferred_element_type=F32)


def kernel(
    emb_in, mem_in, sel_in, out,
    emb, mem, sel, sort, pick, rawx, rawy, raws, s1r, s2s, s2r, s3r, s3s, s4r, chosen,
    points, cands, cov, acc, gs, gy, ts, gz,
    loaded, zsend, xsend, ysend, ksend, psend, wrecv, crecv, gsend, grecv,
):
    x, y, z, k = coords()
    rows, width = emb.shape
    half = width // 2
    scale = 1.0 / math.sqrt(width)
    q = x * 2 + k

    def at(dx=0, dy=0, dz=0, dk=0):
        return device(
            lax.rem(x + dx, 4), lax.rem(y + dy, 4), lax.rem(z + dz, 8), lax.rem(k + dk, 2)
        )

    def at_q(d):
        other = lax.rem(q + d, 8)
        return device(lax.div(other, 2), y, z, lax.rem(other, 2))

    def copy(src, dst, ssem, rsem, to):
        return pltpu.make_async_remote_copy(
            src_ref=src, dst_ref=dst, send_sem=ssem, recv_sem=rsem, device_id=to, device_id_type=MESH
        )

    barrier = pltpu.get_barrier_semaphore()
    peers = [at(dz=d) for d in range(1, 8)] + [at_q(d) for d in range(1, 8)] + [at(dy=d) for d in range(1, 4)]
    for peer in peers:
        pl.semaphore_signal(barrier, inc=1, device_id=peer, device_id_type=MESH)
    loads = [
        pltpu.make_async_copy(src, dst, loaded.at[i])
        for i, (src, dst) in enumerate(((mem_in, mem), (sel_in, sel), (emb_in, emb)))
    ]
    for load in loads:
        load.start()
    for load in loads:
        load.wait()

    win = mem[...]
    up = lax.rem(z - win + 8, 8)
    wave = jnp.where(up == 0, 0, jnp.where(up <= 4, 2 * up - 1, 16 - 2 * up))
    in_wave = lax.broadcasted_iota(I32, (WIN, rows), 0) == wave
    before = lax.broadcasted_iota(I32, (rows, rows), 0) < lax.broadcasted_iota(I32, (rows, rows), 1)
    ahead = jnp.dot(
        jnp.where(in_wave, 1.0, 0.0).astype(BF16), jnp.where(before, 1.0, 0.0).astype(BF16),
        preferred_element_type=F32,
    )
    place = jnp.sum(jnp.where(in_wave, ahead, 0.0), axis=0, keepdims=True).astype(I32)
    slot = wave * CAP + place
    slots = WIN * CAP
    sorter = jnp.where(lax.broadcasted_iota(I32, (slots, rows), 0) == slot, 1.0, 0.0)
    base = (lax.axis_index("row") * 32 + lax.axis_index("col")) * rows
    local = base + lax.broadcasted_iota(I32, (PICKS, rows), 1)
    eye = lax.broadcasted_iota(I32, (PICKS, PICKS), 0) == lax.broadcasted_iota(I32, (PICKS, PICKS), 1)
    pickers = []
    for g in range(WIN):
        ids = jnp.sum(jnp.where(eye, sel[g : g + 1, :].astype(F32), 0.0), axis=1, keepdims=True)
        pickers.append(jnp.where(local == ids.astype(I32), 1.0, 0.0))
    onehot = jnp.concatenate([sorter] + pickers, axis=0).astype(BF16)
    low = jnp.dot(onehot, emb[:, :half], preferred_element_type=F32)
    high = jnp.dot(onehot, emb[:, half:], preferred_element_type=F32)
    for g in range(WIN):
        lo, hi = slots + g * PICKS, slots + (g + 1) * PICKS
        pick[g] = jnp.concatenate([low[lo:hi], high[lo:hi]], axis=0).astype(BF16)
    for n in range(WIN):
        lo, hi = n * CAP, (n + 1) * CAP
        part = jnp.concatenate([low[lo:hi], high[lo:hi]], axis=0).astype(BF16)
        if n == 0:
            rawx[0, 0] = part
        else:
            sort[n - 1] = part
    acc[...] = jnp.zeros_like(acc)

    pl.semaphore_wait(barrier, len(peers))

    def start(cp):
        cp.start()
        return cp

    def sent(ref, sem):
        pltpu.make_async_copy(ref, ref, sem).wait()

    picks1 = []
    for d in range(1, 8):
        g = lax.rem(z - lax.rem(q + d, 8) + 8, 8)
        picks1.append(start(copy(pick.at[g], s1r.at[d - 1], psend.at[0], crecv.at[d - 1], at_q(d))))

    def zcopy(n):
        return start(
            copy(sort.at[n - 1], rawx.at[n, 0], zsend, wrecv.at[n, ZK], at(dz=8 - WAVES[n]))
        )

    wave_copies = {}

    def wcopy(n, kind, src, dst, to):
        sem = xsend if kind in (XP, XM, X3) else ysend if kind in (YP, YM, Y3) else ksend
        wave_copies[n, kind] = start(copy(src, dst, sem, wrecv.at[n, kind], to))

    def level0(n):
        if n > 0:
            zs[n].wait_recv()
        own = rawx.at[n, 0]
        wcopy(n, XP, own, rawx.at[n, 1], at(dx=1))
        wcopy(n, YP, own, rawy.at[n, 0], at(dy=1))
        wcopy(n, XM, own, rawx.at[n, 2], at(dx=3))
        wcopy(n, YM, own, rawy.at[n, 1], at(dy=3))

    def level1(n):
        xk, yk, s, on = (XP, YP, 1, 1) if n % 2 == 0 else (XM, YM, 2, 3)
        wave_copies[n, xk].wait_recv()
        wcopy(n, X3, rawx.at[n, s], rawx.at[n, 3], at(dx=on))
        wave_copies[n, yk].wait_recv()
        wcopy(n, Y3, rawy.at[n, s - 1], rawy.at[n, 2], at(dy=on))
        wave_copies[n, XP + XM - xk].wait_recv()
        wcopy(n, KK, rawx.at[n, pl.ds(0, 3)], raws.at[n, pl.ds(0, 3)], at(dk=1))
        wave_copies[n, YP + YM - yk].wait_recv()

    def level2(n):
        wave_copies[n, X3].wait_recv()
        wcopy(n, KK, rawx.at[n, 3], raws.at[n, 3], at(dk=1))
        wave_copies[n, Y3].wait_recv()

    def level3(n):
        sent(raws.at[n], wrecv.at[n, KK])

    def chosen1():
        total = pick[lax.rem(z - q + 8, 8)].astype(F32)
        for d in range(7):
            picks1[d].wait_recv()
            total = total + s1r[d].astype(F32)
        s2s[...] = total.astype(BF16)
        cp = copy(s2s, s2r, psend.at[1], crecv.at[7], at(dz=8 - q))

        @pl.when(q == 0)
        def _():
            s2r[...] = s2s[...]

        @pl.when(q != 0)
        def _():
            cp.start()

        return cp

    def chosen2(cp):
        @pl.when(q != 0)
        def _():
            cp.wait()

        return [
            start(copy(s2r, s3r.at[d - 1], psend.at[2], crecv.at[7 + d], at(dy=d))) for d in range(1, 4)
        ]

    def chosen3(cps):
        total = s2r[...].astype(F32)
        for d in range(3):
            cps[d].wait_recv()
            total = total + s3r[d].astype(F32)
        s3s[...] = total.astype(BF16)
        return [
            start(copy(s3s, s4r.at[d - 1], psend.at[3], crecv.at[10 + d], at_q(d))) for d in range(1, 8)
        ]

    def chosen4(cps):
        total = s3s[...].astype(F32)
        for d in range(7):
            cps[d].wait_recv()
            total = total + s4r[d].astype(F32)
        whole = jnp.concatenate([total[:PICKS], total[PICKS:]], axis=1)
        chosen[...] = jnp.concatenate([whole, whole], axis=0).astype(BF16)

    pair = 2 * CAP
    prow, crow = 2 * RING * pair, RING * pair

    def assemble(group):
        def put(dst, row, ref, s):
            a, b = ref[2 * group, s].astype(F32), ref[2 * group + 1, s].astype(F32)
            dst[row : row + pair, :half] = jnp.concatenate([a[:CAP], b[:CAP]], axis=0).astype(BF16)
            dst[row : row + pair, half:] = jnp.concatenate([a[CAP:], b[CAP:]], axis=0).astype(BF16)

        for s in range(RING):
            put(points, group * prow + s * pair, rawx, s)
            put(points, group * prow + crow + s * pair, raws, s)
            put(cands, group * crow + s * pair, *((rawx, 0) if s == 0 else (rawy, s - 1)))

    def cover(group):
        near = rows_dot(points[group * prow : (group + 1) * prow, :], chosen[...]) * scale
        cov[group * prow : (group + 1) * prow, :] = jnp.maximum(jnp.max(near, axis=1, keepdims=True), 0.0)

    def unit(a, b):
        lo = pl.multiple_of(a * prow, prow)
        sims = rows_dot(points[pl.ds(lo, prow), :], cands[pl.ds(pl.multiple_of(b * crow, crow), crow), :])
        terms = jnp.maximum(sims * scale - cov[pl.ds(lo, prow), :], 0.0)
        acc[b] += jnp.sum(terms.reshape(prow // 8, 8, crow), axis=0)

    def fold(group):
        cover(group)

        def body(i, carry):
            a = jnp.where(i <= group, group, i - group - 1)
            b = jnp.where(i <= group, i, group)
            unit(a, b)
            return carry

        lax.fori_loop(0, 2 * group + 1, body, 0)

    zs = {n: zcopy(n) for n in (1, 2)}
    level0(0)
    zs.update({n: zcopy(n) for n in (3, 4)})
    level0(1)
    level0(2)
    zs.update({n: zcopy(n) for n in (5, 6)})
    level1(0)
    c2 = chosen1()
    level0(3)
    level0(4)
    zs[7] = zcopy(7)
    level1(1)
    level1(2)
    level2(0)
    c3 = chosen2(c2)
    level0(5)
    level0(6)
    level1(3)
    level1(4)
    level2(1)
    level2(2)
    c4 = chosen3(c3)
    level3(0)
    level3(1)
    assemble(0)
    level0(7)
    level1(5)
    level1(6)
    level2(3)
    level2(4)
    chosen4(c4)
    fold(0)
    level3(2)
    level3(3)
    assemble(1)
    level1(7)
    level2(5)
    level2(6)
    fold(1)
    level3(4)
    level3(5)
    assemble(2)
    level2(7)
    fold(2)
    sent(sort, zsend)
    sent(rawy, xsend)
    sent(rawy, ysend)
    sent(raws, ksend)
    sent(s1r, psend.at[0])
    sent(s3r, psend.at[2])
    sent(s4r, psend.at[3])
    level3(6)
    level3(7)
    assemble(3)
    fold(3)

    groups = WIN // 2
    part = jnp.concatenate(
        [jnp.sum(acc[b], axis=0, keepdims=True) for b in range(groups)] + [jnp.zeros((8 - groups, crow), F32)], axis=0
    )
    gs[...] = jnp.concatenate([part, jnp.zeros((8, 256 - crow), F32)], axis=1)
    back = [start(copy(gs, gy.at[i], gsend.at[0], grecv.at[i], at(dy=d))) for i, d in enumerate((1, 3, 2))]
    total = gs[...]
    for i, s in enumerate((2, 1, 3)):
        back[i].wait_recv()
        total = total + pltpu.roll(gy[i], 256 - s * pair, 1)
    ts[...] = total[:, :128]
    home = [
        start(copy(ts, gz.at[n - 1], gsend.at[1], grecv.at[2 + n], at(dz=WAVES[n]))) for n in range(1, 8)
    ]
    row_id = lax.broadcasted_iota(I32, (8, 128), 0)
    lane = lax.broadcasted_iota(I32, (8, 128), 1)
    shift = lax.rem(wave, 2) * CAP + place
    spread = jnp.where(lax.broadcasted_iota(I32, (128, rows), 0) == shift, 1.0, 0.0)
    gathered = jnp.zeros((8, 128), F32)
    for n in range(8):
        if n > 0:
            home[n - 1].wait_recv()
        got = ts[...] if n == 0 else gz[n - 1]
        first = (n % 2) * CAP
        here = (row_id == n // 2) & (lane >= first) & (lane < first + CAP)
        gathered = gathered + jnp.where(here, got, 0.0)
    placed = jnp.dot(gathered, spread, precision=lax.Precision.HIGHEST, preferred_element_type=F32)
    mine = lax.broadcasted_iota(I32, (8, rows), 0) == lax.div(wave, 2)
    out[...] = jnp.sum(jnp.where(mine, placed, 0.0), axis=0, keepdims=True) * GAIN_SCALE
    sent(gy, gsend.at[0])
    sent(gz, gsend.at[1])


def shards(embeddings, membership, selected):
    rows, width = embeddings.shape
    half = width // 2
    chunk, short = (2 * CAP, half), (2 * PICKS, half)
    dma = pltpu.SemaphoreType.DMA
    gains = pl.pallas_call(
        kernel,
        out_shape=jax.ShapeDtypeStruct((1, rows), F32),
        in_specs=[pl.BlockSpec(memory_space=pltpu.HBM)] * 3,
        out_specs=pl.BlockSpec(memory_space=pltpu.VMEM),
        scratch_shapes=[
            pltpu.VMEM((rows, width), BF16),
            pltpu.VMEM((1, rows), I32),
            pltpu.VMEM(selected.shape, I32),
            pltpu.VMEM((7,) + chunk, BF16),
            pltpu.VMEM((8,) + short, BF16),
            pltpu.VMEM((8, 4) + chunk, BF16),
            pltpu.VMEM((8, 3) + chunk, BF16),
            pltpu.VMEM((8, 4) + chunk, BF16),
            pltpu.VMEM((7,) + short, BF16),
            pltpu.VMEM(short, BF16),
            pltpu.VMEM(short, BF16),
            pltpu.VMEM((3,) + short, BF16),
            pltpu.VMEM(short, BF16),
            pltpu.VMEM((7,) + short, BF16),
            pltpu.VMEM((2 * PICKS, width), BF16),
            pltpu.VMEM((8 * 8 * CAP, width), BF16),
            pltpu.VMEM((8 * 4 * CAP, width), BF16),
            pltpu.VMEM((8 * 8 * CAP, 1), F32),
            pltpu.VMEM((4, 8, 8 * CAP), F32),
            pltpu.VMEM((8, 256), F32),
            pltpu.VMEM((3, 8, 256), F32),
            pltpu.VMEM((8, 128), F32),
            pltpu.VMEM((7, 8, 128), F32),
            dma((3,)), dma, dma, dma, dma, dma((4,)), dma((8, 8)), dma((18,)), dma((2,)), dma((10,)),
        ],
        compiler_params=pltpu.CompilerParams(
            collective_id=0, has_side_effects=True, vmem_limit_bytes=62 * 1024 * 1024
        ),
    )(embeddings, membership.reshape(1, rows), selected)
    return gains.reshape(rows)


def solution(mesh):
    in_specs = (P(("row", "col"), None), P(("row", "col"), None), P())
    out_specs = P(("row", "col"))
    return jax.shard_map(shards, mesh=mesh, in_specs=in_specs, out_specs=out_specs, check_vma=False)
```

```python
import functools
import math

import jax
import jax.numpy as jnp
from jax import lax
from jax.experimental import pallas as pl
from jax.experimental.pallas import tpu as pltpu
from jax.sharding import PartitionSpec as P

GAIN_SCALE = 1.0 / 64.0
MESH = pl.DeviceIdType.MESH
F32, BF16, I32 = jnp.float32, jnp.bfloat16, jnp.int32

CAP = 24
WIN = 8
PICKS = 8
RING = 4
WAVES = (0, 1, 7, 2, 6, 3, 5, 4)
BATCHES = ((0, 1), (1, 2), (3, 2), (5, 2), (7, 1))
PAIRS = ((1, 2), (3, 4), (5, 6), (7, 0))
ZK, XP, XM, X3, YP, YM, Y3, KK = range(8)


def coords():
    row, col = lax.axis_index("row"), lax.axis_index("col")
    x, z_lo = lax.rem(row, 4), lax.div(row, 4)
    z_hi, y, k = lax.div(col, 8), lax.rem(lax.div(col, 2), 4), lax.rem(col, 2)
    return x, y, z_hi * 2 + z_lo, k


def device(x, y, z, k):
    return lax.rem(z, 2) * 4 + x, lax.div(z, 2) * 8 + y * 2 + k


def rows_dot(left, right):
    return lax.dot_general(left, right, (((1,), (1,)), ((), ())), preferred_element_type=F32)


def kernel(
    emb_in, mem_in, sel_in, out,
    emb, mem, sel, sort, pick, rawx, rawy, raws, s1r, s2s, s2r, s3r, s3s, s4r, chosen,
    points, cands, cov, acc, gs, gz,
    loaded, zsend, xsend, ysend, ksend, psend, wrecv, crecv, gsend, grecv,
):
    x, y, z, k = coords()
    rows, width = emb.shape
    half = width // 2
    scale = 1.0 / math.sqrt(width)
    q = x * 2 + k

    def at(dx=0, dy=0, dz=0, dk=0):
        return device(
            lax.rem(x + dx, 4), lax.rem(y + dy, 4), lax.rem(z + dz, 8), lax.rem(k + dk, 2)
        )

    def at_q(d):
        other = lax.rem(q + d, 8)
        return device(lax.div(other, 2), y, z, lax.rem(other, 2))

    def copy(src, dst, ssem, rsem, to):
        return pltpu.make_async_remote_copy(
            src_ref=src, dst_ref=dst, send_sem=ssem, recv_sem=rsem, device_id=to, device_id_type=MESH
        )

    barrier = pltpu.get_barrier_semaphore()
    peers = [at(dz=d) for d in range(1, 8)] + [at_q(d) for d in range(1, 8)] + [at(dy=d) for d in range(1, 4)]
    loads = [
        pltpu.make_async_copy(src, dst, loaded.at[i])
        for i, (src, dst) in enumerate(((mem_in, mem), (sel_in, sel), (emb_in, emb)))
    ]
    for load in loads:
        load.start()
    for peer in peers:
        pl.semaphore_signal(barrier, inc=1, device_id=peer, device_id_type=MESH)
    for load in loads:
        load.wait()

    win = mem[...]
    up = lax.rem(z - win + 8, 8)
    wave = jnp.where(up == 0, 0, jnp.where(up <= 4, 2 * up - 1, 16 - 2 * up))
    in_wave = lax.broadcasted_iota(I32, (WIN, rows), 0) == wave
    before = lax.broadcasted_iota(I32, (rows, rows), 0) < lax.broadcasted_iota(I32, (rows, rows), 1)
    ahead = jnp.dot(
        jnp.where(in_wave, 1.0, 0.0).astype(BF16), jnp.where(before, 1.0, 0.0).astype(BF16),
        preferred_element_type=F32,
    )
    place = jnp.sum(jnp.where(in_wave, ahead, 0.0), axis=0, keepdims=True).astype(I32)
    slot = wave * CAP + place
    slots = WIN * CAP
    sorter = jnp.where(lax.broadcasted_iota(I32, (slots, rows), 0) == slot, 1.0, 0.0)
    base = (lax.axis_index("row") * 32 + lax.axis_index("col")) * rows
    local = base + lax.broadcasted_iota(I32, (PICKS, rows), 1)
    eye = lax.broadcasted_iota(I32, (PICKS, PICKS), 0) == lax.broadcasted_iota(I32, (PICKS, PICKS), 1)
    pickers = []
    for g in range(WIN):
        ids = jnp.sum(jnp.where(eye, sel[g : g + 1, :].astype(F32), 0.0), axis=1, keepdims=True)
        pickers.append(jnp.where(local == ids.astype(I32), 1.0, 0.0))
    onehot = jnp.concatenate([sorter] + pickers, axis=0).astype(BF16)
    low = jnp.dot(onehot, emb[:, :half], preferred_element_type=F32)
    high = jnp.dot(onehot, emb[:, half:], preferred_element_type=F32)
    for g in range(WIN):
        lo, hi = slots + g * PICKS, slots + (g + 1) * PICKS
        pick[g] = jnp.concatenate([low[lo:hi], high[lo:hi]], axis=0).astype(BF16)
    for n in range(WIN):
        lo, hi = n * CAP, (n + 1) * CAP
        part = jnp.concatenate([low[lo:hi], high[lo:hi]], axis=0).astype(BF16)
        if n == 0:
            rawx[0, 0] = part
        else:
            sort[n - 1] = part
    acc[...] = jnp.zeros_like(acc)

    pl.semaphore_wait(barrier, len(peers))

    def start(cp):
        cp.start()
        return cp

    def sent(ref, sem):
        pltpu.make_async_copy(ref, ref, sem).wait()

    for d in range(1, 8):
        g = lax.rem(z - lax.rem(q + d, 8) + 8, 8)
        start(copy(pick.at[g], s1r.at[d - 1], psend.at[0], crecv.at[0], at_q(d)))

    def zcopy(n):
        return start(
            copy(sort.at[n - 1], rawx.at[0, n], zsend, wrecv.at[n, ZK], at(dz=8 - WAVES[n]))
        )

    wave_copies = {}

    def wcopy(c, kind, src, dst, to):
        sem = xsend if kind in (XP, XM, X3) else ysend if kind in (YP, YM, Y3) else ksend
        wave_copies[c, kind] = start(copy(src, dst, sem, wrecv.at[c, kind], to))

    def span(c):
        return pl.ds(*BATCHES[c])

    def level0(c):
        first, count = BATCHES[c]
        for n in range(first, first + count):
            if n > 0:
                zs[n].wait_recv()
        own = rawx.at[0, span(c)]
        wcopy(c, XP, own, rawx.at[1, span(c)], at(dx=1))
        wcopy(c, YP, own, rawy.at[0, span(c)], at(dy=1))
        wcopy(c, XM, own, rawx.at[2, span(c)], at(dx=3))
        wcopy(c, YM, own, rawy.at[1, span(c)], at(dy=3))

    def level1(c):
        xk, yk, s, on = (XP, YP, 1, 1) if c % 2 == 0 else (XM, YM, 2, 3)
        wave_copies[c, xk].wait_recv()
        wcopy(c, X3, rawx.at[s, span(c)], rawx.at[3, span(c)], at(dx=on))
        wave_copies[c, yk].wait_recv()
        wcopy(c, Y3, rawy.at[s - 1, span(c)], rawy.at[2, span(c)], at(dy=on))
        wave_copies[c, XP + XM - xk].wait_recv()
        wcopy(c, KK, rawx.at[pl.ds(0, 3), span(c)], raws.at[pl.ds(0, 3), span(c)], at(dk=1))
        wave_copies[c, YP + YM - yk].wait_recv()

    def level2(c):
        wave_copies[c, X3].wait_recv()
        wcopy(c, KK, rawx.at[3, span(c)], raws.at[3, span(c)], at(dk=1))
        wave_copies[c, Y3].wait_recv()

    def level3(c):
        sent(raws.at[:, span(c)], wrecv.at[c, KK])

    def chosen1():
        sent(s1r, crecv.at[0])
        total = pick[lax.rem(z - q + 8, 8)].astype(F32) + jnp.sum(s1r[...].astype(F32), axis=0)
        s2s[...] = total.astype(BF16)

        @pl.when(q == 0)
        def _():
            s2r[...] = s2s[...]

        @pl.when(q != 0)
        def _():
            copy(s2s, s2r, psend.at[1], crecv.at[1], at(dz=8 - q)).start()

    def chosen2():
        @pl.when(q != 0)
        def _():
            copy(s2s, s2r, psend.at[1], crecv.at[1], at(dz=8 - q)).wait()

        for d in range(1, 4):
            start(copy(s2r, s3r.at[d - 1], psend.at[2], crecv.at[2], at(dy=d)))

    def chosen3():
        sent(s3r, crecv.at[2])
        total = s2r[...].astype(F32) + jnp.sum(s3r[...].astype(F32), axis=0)
        s3s[...] = total.astype(BF16)
        for d in range(1, 8):
            start(copy(s3s, s4r.at[d - 1], psend.at[3], crecv.at[3], at_q(d)))

    def chosen4():
        sent(s4r, crecv.at[3])
        total = s3s[...].astype(F32) + jnp.sum(s4r[...].astype(F32), axis=0)
        whole = jnp.concatenate([total[:PICKS], total[PICKS:]], axis=1)
        chosen[...] = jnp.concatenate([whole, whole], axis=0).astype(BF16)

    pair = 2 * CAP
    prow, crow = 2 * RING * pair, RING * pair

    def assemble(group):
        def put(dst, row, ref, s):
            a, b = ref[s, PAIRS[group][0]].astype(F32), ref[s, PAIRS[group][1]].astype(F32)
            dst[row : row + pair, :half] = jnp.concatenate([a[:CAP], b[:CAP]], axis=0).astype(BF16)
            dst[row : row + pair, half:] = jnp.concatenate([a[CAP:], b[CAP:]], axis=0).astype(BF16)

        for s in range(RING):
            put(points, group * prow + s * pair, rawx, s)
            put(points, group * prow + crow + s * pair, raws, s)
            put(cands, group * crow + s * pair, *((rawx, 0) if s == 0 else (rawy, s - 1)))

    def cover(group):
        near = rows_dot(points[group * prow : (group + 1) * prow, :], chosen[...]) * scale
        cov[group * prow : (group + 1) * prow, :] = jnp.maximum(jnp.max(near, axis=1, keepdims=True), 0.0)

    last = WIN // 2 - 1
    old_rows, old_cands = last * prow, last * crow

    def block(lo, count, left, right):
        cand = cands[left:right, :]
        terms = jnp.maximum(rows_dot(points[pl.ds(lo, count), :], cand) * scale - cov[pl.ds(lo, count), :], 0.0)
        summed = jnp.sum(terms.reshape(count // 8, 8, right - left), axis=0)
        for b in range(left // crow, right // crow):
            acc[b] += summed[:, b * crow - left : (b + 1) * crow - left]

    def fold_old():
        for group in range(last):
            cover(group)

        def body(i, carry):
            block(pl.multiple_of(i * prow, prow), prow, 0, old_cands)
            return carry

        lax.fori_loop(0, last, body, 0)

    def fold_last():
        block(0, old_rows, old_cands, old_cands + crow)
        cover(last)
        block(old_rows, prow, 0, old_cands + crow)

    zs = {n: zcopy(n) for n in (1, 2)}
    level0(0)
    zs.update({n: zcopy(n) for n in (3, 4)})
    level0(1)
    zs.update({n: zcopy(n) for n in (5, 6)})
    chosen1()
    level1(0)
    level0(2)
    zs[7] = zcopy(7)
    level1(1)
    level2(0)
    chosen2()
    level0(3)
    level1(2)
    level2(1)
    chosen3()
    level3(0)
    level3(1)
    assemble(0)
    level0(4)
    level1(3)
    level2(2)
    level3(2)
    assemble(1)
    chosen4()
    level2(3)
    level1(4)
    level3(3)
    assemble(2)
    fold_old()
    level2(4)
    sent(sort, zsend)
    sent(rawy, xsend)
    sent(rawy, ysend)
    sent(raws, ksend)
    sent(s1r, psend.at[0])
    sent(s3r, psend.at[2])
    sent(s4r, psend.at[3])
    level3(4)
    assemble(3)
    fold_last()

    for b in range(WIN // 2):
        part = jnp.sum(acc[b], axis=0, keepdims=True)
        gs[b] = jnp.concatenate([part, jnp.zeros((1, 256 - crow), F32)], axis=1)
    steps = (0, 1, 3, 2)
    for i, dy in enumerate(steps):
        for n in range(WIN):
            if i == n == 0:
                gz[0] = gs[WIN // 2 - 1]
            else:
                start(copy(gs.at[(n + 7) % 8 // 2], gz.at[i * WIN + n], gsend, grecv, at(dy=dy, dz=WAVES[n])))
    shift = lax.rem(wave + 1, 2) * CAP + place
    spread = jnp.where(lax.broadcasted_iota(I32, (128, rows), 0) == shift, 1.0, 0.0)
    mine = lax.broadcasted_iota(I32, (WIN, rows), 0) == wave
    sent(gz.at[pl.ds(1, 31)], grecv)
    total = gz[0:WIN].reshape(WIN, 256)
    for i, s in ((1, 2), (2, 1), (3, 3)):
        total = total + pltpu.roll(gz[i * WIN : (i + 1) * WIN].reshape(WIN, 256), 256 - s * pair, 1)
    placed = jnp.dot(total[:, :128], spread, precision=lax.Precision.HIGHEST, preferred_element_type=F32)
    out[...] = jnp.sum(jnp.where(mine, placed, 0.0), axis=0, keepdims=True) * GAIN_SCALE
    sent(gz.at[pl.ds(1, 31)], gsend)


def shards(embeddings, membership, selected):
    rows, width = embeddings.shape
    half = width // 2
    chunk, short = (2 * CAP, half), (2 * PICKS, half)
    dma = pltpu.SemaphoreType.DMA
    gains = pl.pallas_call(
        kernel,
        out_shape=jax.ShapeDtypeStruct((1, rows), F32),
        in_specs=[pl.BlockSpec(memory_space=pltpu.HBM)] * 3,
        out_specs=pl.BlockSpec(memory_space=pltpu.VMEM),
        scratch_shapes=[
            pltpu.VMEM((rows, width), BF16),
            pltpu.VMEM((1, rows), I32),
            pltpu.VMEM(selected.shape, I32),
            pltpu.VMEM((7,) + chunk, BF16),
            pltpu.VMEM((8,) + short, BF16),
            pltpu.VMEM((4, 8) + chunk, BF16),
            pltpu.VMEM((3, 8) + chunk, BF16),
            pltpu.VMEM((4, 8) + chunk, BF16),
            pltpu.VMEM((7,) + short, BF16),
            pltpu.VMEM(short, BF16),
            pltpu.VMEM(short, BF16),
            pltpu.VMEM((3,) + short, BF16),
            pltpu.VMEM(short, BF16),
            pltpu.VMEM((7,) + short, BF16),
            pltpu.VMEM((2 * PICKS, width), BF16),
            pltpu.VMEM((8 * 8 * CAP, width), BF16),
            pltpu.VMEM((8 * 4 * CAP, width), BF16),
            pltpu.VMEM((8 * 8 * CAP, 1), F32),
            pltpu.VMEM((4, 8, 8 * CAP), F32),
            pltpu.VMEM((4, 1, 256), F32),
            pltpu.VMEM((32, 1, 256), F32),
            dma((3,)), dma, dma, dma, dma, dma((4,)), dma((8, 8)), dma((4,)), dma, dma,
        ],
        compiler_params=pltpu.CompilerParams(
            collective_id=0, has_side_effects=True, vmem_limit_bytes=62 * 1024 * 1024
        ),
    )(embeddings, membership.reshape(1, rows), selected)
    return gains.reshape(rows)


def solution(mesh):
    in_specs = (P(("row", "col"), None), P(("row", "col"), None), P())
    out_specs = P(("row", "col"))
    return jax.shard_map(shards, mesh=mesh, in_specs=in_specs, out_specs=out_specs, check_vma=False)
```

```python
import functools
import math

import jax
import jax.numpy as jnp
from jax import lax
from jax.experimental import pallas as pl
from jax.experimental.pallas import tpu as pltpu
from jax.sharding import PartitionSpec as P

GAIN_SCALE = 1.0 / 64.0
MESH = pl.DeviceIdType.MESH
F32, BF16, I32 = jnp.float32, jnp.bfloat16, jnp.int32

CAP = 24
WIN = 8
PICKS = 8
RING = 4
WAVES = (0, 1, 7, 2, 6, 3, 5, 4)
BATCHES = ((0, 1), (1, 2), (3, 2), (5, 2), (7, 1))
PAIRS = ((1, 2), (3, 4), (5, 6), (7, 0))
ZK, XP, XM, X3, YP, YM, Y3, KK = range(8)


def coords():
    row, col = lax.axis_index("row"), lax.axis_index("col")
    x, z_lo = lax.rem(row, 4), lax.div(row, 4)
    z_hi, y, k = lax.div(col, 8), lax.rem(lax.div(col, 2), 4), lax.rem(col, 2)
    return x, y, z_hi * 2 + z_lo, k


def device(x, y, z, k):
    return lax.rem(z, 2) * 4 + x, lax.div(z, 2) * 8 + y * 2 + k


def rows_dot(left, right):
    return lax.dot_general(left, right, (((1,), (1,)), ((), ())), preferred_element_type=F32)


def kernel(
    emb_in, mem_in, sel_in, out,
    emb, mem, sel, sort, pick, rawx, rawy, raws, s1r, s1s, s2x, s2s, s2r, s3r, s3s, s4r, s5s, s5r, chosen,
    points, cands, cov, acc, gs, gz,
    loaded, zsend, xsend, ysend, ksend, psend, wrecv, crecv, gsend, grecv,
):
    x, y, z, k = coords()
    rows, width = emb.shape
    half = width // 2
    scale = 1.0 / math.sqrt(width)
    q = x * 2 + k

    def at(dx=0, dy=0, dz=0, dk=0):
        return device(
            lax.rem(x + dx, 4), lax.rem(y + dy, 4), lax.rem(z + dz, 8), lax.rem(k + dk, 2)
        )

    def copy(src, dst, ssem, rsem, to):
        return pltpu.make_async_remote_copy(
            src_ref=src, dst_ref=dst, send_sem=ssem, recv_sem=rsem, device_id=to, device_id_type=MESH
        )

    barrier = pltpu.get_barrier_semaphore()
    peers = [at(dz=d) for d in range(1, 8)] + [at(dk=1)]
    peers += [at(dx=d) for d in range(1, 4)] + [at(dy=d) for d in range(1, 4)]
    loads = [
        pltpu.make_async_copy(src, dst, loaded.at[i])
        for i, (src, dst) in enumerate(((mem_in, mem), (sel_in, sel), (emb_in, emb)))
    ]
    for load in loads:
        load.start()
    for peer in peers:
        pl.semaphore_signal(barrier, inc=1, device_id=peer, device_id_type=MESH)
    for load in loads:
        load.wait()

    win = mem[...]
    up = lax.rem(z - win + 8, 8)
    wave = jnp.where(up == 0, 0, jnp.where(up <= 4, 2 * up - 1, 16 - 2 * up))
    in_wave = lax.broadcasted_iota(I32, (WIN, rows), 0) == wave
    before = lax.broadcasted_iota(I32, (rows, rows), 0) < lax.broadcasted_iota(I32, (rows, rows), 1)
    ahead = jnp.dot(
        jnp.where(in_wave, 1.0, 0.0).astype(BF16), jnp.where(before, 1.0, 0.0).astype(BF16),
        preferred_element_type=F32,
    )
    place = jnp.sum(jnp.where(in_wave, ahead, 0.0), axis=0, keepdims=True).astype(I32)
    slot = wave * CAP + place
    slots = WIN * CAP
    sorter = jnp.where(lax.broadcasted_iota(I32, (slots, rows), 0) == slot, 1.0, 0.0)
    base = (lax.axis_index("row") * 32 + lax.axis_index("col")) * rows
    local = base + lax.broadcasted_iota(I32, (PICKS, rows), 1)
    eye = lax.broadcasted_iota(I32, (PICKS, PICKS), 0) == lax.broadcasted_iota(I32, (PICKS, PICKS), 1)
    pickers = []
    for i in range(WIN):
        g = lax.rem(z + 8 - ((i % 4) * 2 + i // 4), 8)
        ids = jnp.sum(jnp.where(eye, sel[pl.ds(g, 1), :].astype(F32), 0.0), axis=1, keepdims=True)
        pickers.append(jnp.where(local == ids.astype(I32), 1.0, 0.0))
    onehot = jnp.concatenate([sorter] + pickers, axis=0).astype(BF16)
    low = jnp.dot(onehot, emb[:, :half], preferred_element_type=F32)
    high = jnp.dot(onehot, emb[:, half:], preferred_element_type=F32)
    for g in range(WIN):
        lo, hi = slots + g * PICKS, slots + (g + 1) * PICKS
        pick[g // 4, g % 4] = jnp.concatenate([low[lo:hi], high[lo:hi]], axis=0).astype(BF16)
    for n in range(WIN):
        lo, hi = n * CAP, (n + 1) * CAP
        part = jnp.concatenate([low[lo:hi], high[lo:hi]], axis=0).astype(BF16)
        if n == 0:
            rawx[0, 0] = part
        else:
            sort[n - 1] = part
    acc[...] = jnp.zeros_like(acc)

    pl.semaphore_wait(barrier, len(peers))

    def start(cp):
        cp.start()
        return cp

    def sent(ref, sem):
        pltpu.make_async_copy(ref, ref, sem).wait()

    start(copy(pick.at[1 - k], s1r, psend.at[0], crecv.at[0], at(dk=1)))

    def zcopy(n):
        return start(
            copy(sort.at[n - 1], rawx.at[0, n], zsend, wrecv.at[n, ZK], at(dz=8 - WAVES[n]))
        )

    wave_copies = {}

    def wcopy(c, kind, src, dst, to):
        sem = xsend if kind in (XP, XM, X3) else ysend if kind in (YP, YM, Y3) else ksend
        wave_copies[c, kind] = start(copy(src, dst, sem, wrecv.at[c, kind], to))

    def span(c):
        return pl.ds(*BATCHES[c])

    def level0(c):
        first, count = BATCHES[c]
        for n in range(first, first + count):
            if n > 0:
                zs[n].wait_recv()
        own = rawx.at[0, span(c)]
        wcopy(c, XP, own, rawx.at[1, span(c)], at(dx=1))
        wcopy(c, YP, own, rawy.at[0, span(c)], at(dy=1))
        wcopy(c, XM, own, rawx.at[2, span(c)], at(dx=3))
        wcopy(c, YM, own, rawy.at[1, span(c)], at(dy=3))
        if c == len(BATCHES) - 1:
            start(copy(own, rawx.at[3, span(c)], xsend, wrecv.at[c, X3], at(dx=2)))
            start(copy(own, rawy.at[2, span(c)], ysend, wrecv.at[c, Y3], at(dy=2)))

    def level1(c):
        first, count = BATCHES[c]
        for kx, ky, s, on in ((XP, YP, 1, 1), (XM, YM, 2, 3)):
            far = [n for n in range(first, first + count) if n % 2 == s % 2 and c < len(BATCHES) - 1]
            wave_copies[c, kx].wait_recv()
            for n in far:
                start(copy(rawx.at[s, n], rawx.at[3, n], xsend, wrecv.at[c, X3], at(dx=on)))
            wave_copies[c, ky].wait_recv()
            for n in far:
                start(copy(rawy.at[s - 1, n], rawy.at[2, n], ysend, wrecv.at[c, Y3], at(dy=on)))
        wcopy(c, KK, rawx.at[pl.ds(0, 3), span(c)], raws.at[pl.ds(0, 3), span(c)], at(dk=1))

    def level2(c):
        sent(rawx.at[3, span(c)], wrecv.at[c, X3])
        wcopy(c, KK, rawx.at[3, span(c)], raws.at[3, span(c)], at(dk=1))
        sent(rawy.at[2, span(c)], wrecv.at[c, Y3])

    def level3(c):
        sent(raws.at[:, span(c)], wrecv.at[c, KK])

    def chosen0():
        sent(s1r, crecv.at[0])
        s1s[...] = (pick[k].astype(F32) + s1r[...].astype(F32)).astype(BF16)
        for d in range(1, 4):
            start(copy(s1s.at[lax.rem(x + d, 4)], s2x.at[d - 1], psend.at[4], crecv.at[4], at(dx=d)))

    def chosen1():
        sent(s2x, crecv.at[4])
        total = s1s[x].astype(F32) + jnp.sum(s2x[...].astype(F32), axis=0)
        s2s[...] = total.astype(BF16)

        @pl.when(q == 0)
        def _():
            s2r[...] = s2s[...]

        @pl.when(q != 0)
        def _():
            copy(s2s, s2r, psend.at[1], crecv.at[1], at(dz=8 - q)).start()

    def chosen2():
        @pl.when(q != 0)
        def _():
            copy(s2s, s2r, psend.at[1], crecv.at[1], at(dz=8 - q)).wait()

        for d in range(1, 4):
            start(copy(s2r, s3r.at[d - 1], psend.at[2], crecv.at[2], at(dx=d)))

    def chosen3():
        sent(s3r, crecv.at[2])
        total = s2r[...].astype(F32) + jnp.sum(s3r[...].astype(F32), axis=0)
        s3s[...] = total.astype(BF16)
        for d in range(1, 4):
            start(copy(s3s, s4r.at[d - 1], psend.at[3], crecv.at[3], at(dy=d)))

    def chosen4():
        sent(s4r, crecv.at[3])
        total = s3s[...].astype(F32) + jnp.sum(s4r[...].astype(F32), axis=0)
        s5s[...] = total.astype(BF16)
        start(copy(s5s, s5r, psend.at[5], crecv.at[5], at(dk=1)))

    def chosen5():
        sent(s5r, crecv.at[5])
        total = s5s[...].astype(F32) + s5r[...].astype(F32)
        whole = jnp.concatenate([total[:PICKS], total[PICKS:]], axis=1)
        chosen[...] = jnp.concatenate([whole, whole], axis=0).astype(BF16)

    pair = 2 * CAP
    prow, crow = 2 * RING * pair, RING * pair

    def assemble(group):
        def put(dst, row, ref, s):
            a, b = ref[s, PAIRS[group][0]].astype(F32), ref[s, PAIRS[group][1]].astype(F32)
            dst[row : row + pair, :half] = jnp.concatenate([a[:CAP], b[:CAP]], axis=0).astype(BF16)
            dst[row : row + pair, half:] = jnp.concatenate([a[CAP:], b[CAP:]], axis=0).astype(BF16)

        for s in range(RING):
            put(points, group * prow + s * pair, rawx, s)
            put(points, group * prow + crow + s * pair, raws, s)
            put(cands, group * crow + s * pair, *((rawx, 0) if s == 0 else (rawy, s - 1)))

    def cover(group):
        near = rows_dot(points[group * prow : (group + 1) * prow, :], chosen[...]) * scale
        cov[group * prow : (group + 1) * prow, :] = jnp.maximum(jnp.max(near, axis=1, keepdims=True), 0.0)

    def block(lo, count, left, right):
        cand = cands[left:right, :]
        terms = jnp.maximum(rows_dot(points[pl.ds(lo, count), :], cand) * scale - cov[pl.ds(lo, count), :], 0.0)
        summed = jnp.sum(terms.reshape(count // 8, 8, right - left), axis=0)
        for b in range(left // crow, right // crow):
            acc[b] += summed[:, b * crow - left : (b + 1) * crow - left]

    def fold(p0, p1, c0, c1):
        block(p0 * prow, (p1 - p0) * prow, c0 * crow, c1 * crow)

    zs = {}
    zs[1] = zcopy(1)
    zs[2] = zcopy(2)
    level0(0)
    chosen0()
    zs[3] = zcopy(3)
    zs[4] = zcopy(4)
    level0(1)
    zs[5] = zcopy(5)
    zs[6] = zcopy(6)
    level1(0)
    level0(2)
    chosen1()
    zs[7] = zcopy(7)
    level1(1)
    level2(0)
    level0(3)
    chosen2()
    level1(2)
    level2(1)
    level3(0)
    level3(1)
    assemble(0)
    level0(4)
    chosen3()
    level1(3)
    level2(2)
    chosen4()
    level3(2)
    assemble(1)
    level2(3)
    level1(4)
    level2(4)
    chosen5()
    cover(0)
    cover(1)
    fold(0, 2, 0, 2)
    level3(3)
    assemble(2)
    cover(2)
    fold(2, 3, 0, 3)
    fold(0, 2, 2, 3)
    level3(4)
    assemble(3)
    fold(0, 3, 3, 4)
    cover(3)
    fold(3, 4, 0, 4)

    for b in range(WIN // 2):
        part = jnp.sum(acc[b], axis=0, keepdims=True)
        gs[b] = jnp.concatenate([part, jnp.zeros((1, 256 - crow), F32)], axis=1)
    steps = (0, 1, 3, 2)
    for n in reversed(range(WIN)):
        for i, dy in reversed(list(enumerate(steps))):
            if i == n == 0:
                gz[0] = gs[WIN // 2 - 1]
            else:
                start(copy(gs.at[(n + 7) % 8 // 2], gz.at[i * WIN + n], gsend, grecv, at(dy=dy, dz=WAVES[n])))
    shift = lax.rem(wave + 1, 2) * CAP + place
    spread = jnp.where(lax.broadcasted_iota(I32, (128, rows), 0) == shift, 1.0, 0.0)
    mine = lax.broadcasted_iota(I32, (WIN, rows), 0) == wave
    sent(sort, zsend)
    sent(rawy, xsend)
    sent(rawy, ysend)
    sent(raws, ksend)
    sent(s1r, psend.at[0])
    sent(s3r, psend.at[2])
    sent(s4r, psend.at[3])
    sent(s2x, psend.at[4])
    sent(s5r, psend.at[5])
    sent(gz.at[pl.ds(1, 31)], grecv)
    total = gz[0:WIN].reshape(WIN, 256)
    for i, s in ((1, 2), (2, 1), (3, 3)):
        total = total + pltpu.roll(gz[i * WIN : (i + 1) * WIN].reshape(WIN, 256), 256 - s * pair, 1)
    placed = jnp.dot(total[:, :128], spread, precision=lax.Precision.HIGHEST, preferred_element_type=F32)
    out[...] = jnp.sum(jnp.where(mine, placed, 0.0), axis=0, keepdims=True) * GAIN_SCALE
    sent(gz.at[pl.ds(1, 31)], gsend)


def shards(embeddings, membership, selected):
    rows, width = embeddings.shape
    half = width // 2
    chunk, short = (2 * CAP, half), (2 * PICKS, half)
    dma = pltpu.SemaphoreType.DMA
    gains = pl.pallas_call(
        kernel,
        out_shape=jax.ShapeDtypeStruct((1, rows), F32),
        in_specs=[pl.BlockSpec(memory_space=pltpu.HBM)] * 3,
        out_specs=pl.BlockSpec(memory_space=pltpu.VMEM),
        scratch_shapes=[
            pltpu.VMEM((rows, width), BF16),
            pltpu.VMEM((1, rows), I32),
            pltpu.VMEM(selected.shape, I32),
            pltpu.VMEM((7,) + chunk, BF16),
            pltpu.VMEM((2, 4) + short, BF16),
            pltpu.VMEM((4, 8) + chunk, BF16),
            pltpu.VMEM((3, 8) + chunk, BF16),
            pltpu.VMEM((4, 8) + chunk, BF16),
            pltpu.VMEM((4,) + short, BF16),
            pltpu.VMEM((4,) + short, BF16),
            pltpu.VMEM((3,) + short, BF16),
            pltpu.VMEM(short, BF16),
            pltpu.VMEM(short, BF16),
            pltpu.VMEM((3,) + short, BF16),
            pltpu.VMEM(short, BF16),
            pltpu.VMEM((3,) + short, BF16),
            pltpu.VMEM(short, BF16),
            pltpu.VMEM(short, BF16),
            pltpu.VMEM((2 * PICKS, width), BF16),
            pltpu.VMEM((8 * 8 * CAP, width), BF16),
            pltpu.VMEM((8 * 4 * CAP, width), BF16),
            pltpu.VMEM((8 * 8 * CAP, 1), F32),
            pltpu.VMEM((4, 8, 8 * CAP), F32),
            pltpu.VMEM((4, 1, 256), F32),
            pltpu.VMEM((32, 1, 256), F32),
            dma((3,)), dma, dma, dma, dma, dma((6,)), dma((8, 8)), dma((6,)), dma, dma,
        ],
        compiler_params=pltpu.CompilerParams(
            collective_id=0, has_side_effects=True, vmem_limit_bytes=62 * 1024 * 1024
        ),
    )(embeddings, membership.reshape(1, rows), selected)
    return gains.reshape(rows)


def solution(mesh):
    in_specs = (P(("row", "col"), None), P(("row", "col"), None), P())
    out_specs = P(("row", "col"))
    return jax.shard_map(shards, mesh=mesh, in_specs=in_specs, out_specs=out_specs, check_vma=False)
```

```python
import functools
import math

import jax
import jax.numpy as jnp
from jax import lax
from jax.experimental import pallas as pl
from jax.experimental.pallas import tpu as pltpu
from jax.sharding import PartitionSpec as P

GAIN_SCALE = 1.0 / 64.0
MESH = pl.DeviceIdType.MESH
F32, BF16, I32 = jnp.float32, jnp.bfloat16, jnp.int32

CAP = 24
WIN = 8
PICKS = 8
RING = 4
WAVES = (0, 1, 7, 2, 6, 3, 5, 4)
BATCHES = ((0, 1), (1, 2), (3, 2), (5, 2), (7, 1))
PAIRS = ((1, 2), (3, 4), (5, 6), (7, 0))
ZK, XP, XM, X3, YP, YM, Y3, KK = range(8)


def coords():
    row, col = lax.axis_index("row"), lax.axis_index("col")
    x, z_lo = lax.rem(row, 4), lax.div(row, 4)
    z_hi, y, k = lax.div(col, 8), lax.rem(lax.div(col, 2), 4), lax.rem(col, 2)
    return x, y, z_hi * 2 + z_lo, k


def device(x, y, z, k):
    return lax.rem(z, 2) * 4 + x, lax.div(z, 2) * 8 + y * 2 + k


def rows_dot(left, right):
    return lax.dot_general(left, right, (((1,), (1,)), ((), ())), preferred_element_type=F32)


def kernel(
    emb_in, mem_in, sel_in, out,
    emb, mem, sel, sort, pick, rawx, rawy, raws, s1r, s1s, s2x, s2s, s2r, s3r, s3s, s4r, s5s, s5r, chosen,
    points, cands, cov, gs, gz,
    loaded, zsend, xsend, ysend, ksend, psend, wrecv, crecv, gsend, grecv,
):
    x, y, z, k = coords()
    rows, width = emb.shape
    half = width // 2
    scale = 1.0 / math.sqrt(width)
    q = x * 2 + k

    def at(dx=0, dy=0, dz=0, dk=0):
        return device(
            lax.rem(x + dx, 4), lax.rem(y + dy, 4), lax.rem(z + dz, 8), lax.rem(k + dk, 2)
        )

    def copy(src, dst, ssem, rsem, to):
        return pltpu.make_async_remote_copy(
            src_ref=src, dst_ref=dst, send_sem=ssem, recv_sem=rsem, device_id=to, device_id_type=MESH
        )

    barrier = pltpu.get_barrier_semaphore()
    peers = [at(dz=d) for d in range(1, 8)] + [at(dk=1)]
    peers += [at(dx=d) for d in range(1, 4)] + [at(dy=d) for d in range(1, 4)]
    loads = [
        pltpu.make_async_copy(src, dst, loaded.at[i])
        for i, (src, dst) in enumerate(((mem_in, mem), (sel_in, sel), (emb_in, emb)))
    ]
    for load in loads:
        load.start()
    for peer in peers:
        pl.semaphore_signal(barrier, inc=1, device_id=peer, device_id_type=MESH)
    for load in loads:
        load.wait()

    win = mem[...]
    up = lax.rem(z - win + 8, 8)
    wave = jnp.where(up == 0, 0, jnp.where(up <= 4, 2 * up - 1, 16 - 2 * up))
    in_wave = lax.broadcasted_iota(I32, (WIN, rows), 0) == wave
    before = lax.broadcasted_iota(I32, (rows, rows), 0) < lax.broadcasted_iota(I32, (rows, rows), 1)
    ahead = jnp.dot(
        jnp.where(in_wave, 1.0, 0.0).astype(BF16), jnp.where(before, 1.0, 0.0).astype(BF16),
        preferred_element_type=F32,
    )
    place = jnp.sum(jnp.where(in_wave, ahead, 0.0), axis=0, keepdims=True).astype(I32)
    slot = wave * CAP + place
    slots = WIN * CAP
    sorter = jnp.where(lax.broadcasted_iota(I32, (slots, rows), 0) == slot, 1.0, 0.0)
    base = (lax.axis_index("row") * 32 + lax.axis_index("col")) * rows
    local = base + lax.broadcasted_iota(I32, (PICKS, rows), 1)
    eye = lax.broadcasted_iota(I32, (PICKS, PICKS), 0) == lax.broadcasted_iota(I32, (PICKS, PICKS), 1)
    pickers = []
    for i in range(WIN):
        g = lax.rem(z + 8 - ((i % 4) * 2 + i // 4), 8)
        ids = jnp.sum(jnp.where(eye, sel[pl.ds(g, 1), :].astype(F32), 0.0), axis=1, keepdims=True)
        pickers.append(jnp.where(local == ids.astype(I32), 1.0, 0.0))

    def moved(parts):
        onehot = jnp.concatenate(parts, axis=0).astype(BF16)
        low = jnp.dot(onehot, emb[:, :half], preferred_element_type=F32)
        return low, jnp.dot(onehot, emb[:, half:], preferred_element_type=F32)

    def sort_waves(*waves):
        low, high = moved([sorter[n * CAP : (n + 1) * CAP] for n in waves])
        for i, n in enumerate(waves):
            lo, hi = i * CAP, (i + 1) * CAP
            part = jnp.concatenate([low[lo:hi], high[lo:hi]], axis=0).astype(BF16)
            if n == 0:
                rawx[0, 0] = part
            else:
                sort[n - 1] = part

    def sort_picks():
        low, high = moved(pickers)
        for g in range(WIN):
            lo, hi = g * PICKS, (g + 1) * PICKS
            pick[g // 4, g % 4] = jnp.concatenate([low[lo:hi], high[lo:hi]], axis=0).astype(BF16)
        start(copy(pick.at[1 - k], s1r, psend.at[0], crecv.at[0], at(dk=1)))

    sort_waves(1, 2)
    pl.semaphore_wait(barrier, len(peers))

    def start(cp):
        cp.start()
        return cp

    def sent(ref, sem):
        pltpu.make_async_copy(ref, ref, sem).wait()

    def zcopy(n):
        return start(
            copy(sort.at[n - 1], rawx.at[0, n], zsend, wrecv.at[n, ZK], at(dz=8 - WAVES[n]))
        )

    wave_copies = {}

    def wcopy(c, kind, src, dst, to):
        sem = xsend if kind in (XP, XM, X3) else ysend if kind in (YP, YM, Y3) else ksend
        wave_copies[c, kind] = start(copy(src, dst, sem, wrecv.at[c, kind], to))

    def span(c):
        return pl.ds(*BATCHES[c])

    def level0(c):
        first, count = BATCHES[c]
        for n in range(first, first + count):
            if n > 0:
                zs[n].wait_recv()
        own = rawx.at[0, span(c)]
        wcopy(c, XP, own, rawx.at[1, span(c)], at(dx=1))
        wcopy(c, YP, own, rawy.at[0, span(c)], at(dy=1))
        wcopy(c, XM, own, rawx.at[2, span(c)], at(dx=3))
        wcopy(c, YM, own, rawy.at[1, span(c)], at(dy=3))
        if c == len(BATCHES) - 1:
            start(copy(own, rawx.at[3, span(c)], xsend, wrecv.at[c, X3], at(dx=2)))
            start(copy(own, rawy.at[2, span(c)], ysend, wrecv.at[c, Y3], at(dy=2)))

    def level1(c):
        first, count = BATCHES[c]
        for kx, ky, s, on in ((XP, YP, 1, 1), (XM, YM, 2, 3)):
            far = [n for n in range(first, first + count) if n % 2 == s % 2 and c < len(BATCHES) - 1]
            wave_copies[c, kx].wait_recv()
            for n in far:
                start(copy(rawx.at[s, n], rawx.at[3, n], xsend, wrecv.at[c, X3], at(dx=on)))
            wave_copies[c, ky].wait_recv()
            for n in far:
                start(copy(rawy.at[s - 1, n], rawy.at[2, n], ysend, wrecv.at[c, Y3], at(dy=on)))
        wcopy(c, KK, rawx.at[pl.ds(0, 3), span(c)], raws.at[pl.ds(0, 3), span(c)], at(dk=1))

    def level2(c):
        sent(rawx.at[3, span(c)], wrecv.at[c, X3])
        wcopy(c, KK, rawx.at[3, span(c)], raws.at[3, span(c)], at(dk=1))
        sent(rawy.at[2, span(c)], wrecv.at[c, Y3])

    def level3(c):
        sent(raws.at[:, span(c)], wrecv.at[c, KK])

    def chosen0():
        sent(s1r, crecv.at[0])
        s1s[...] = (pick[k].astype(F32) + s1r[...].astype(F32)).astype(BF16)
        for d in range(1, 4):
            start(copy(s1s.at[lax.rem(x + d, 4)], s2x.at[d - 1], psend.at[4], crecv.at[4], at(dx=d)))

    def chosen1():
        sent(s2x, crecv.at[4])
        total = s1s[x].astype(F32) + jnp.sum(s2x[...].astype(F32), axis=0)
        s2s[...] = total.astype(BF16)

        @pl.when(q == 0)
        def _():
            s2r[...] = s2s[...]

        @pl.when(q != 0)
        def _():
            copy(s2s, s2r, psend.at[1], crecv.at[1], at(dz=8 - q)).start()

    def chosen2():
        @pl.when(q != 0)
        def _():
            copy(s2s, s2r, psend.at[1], crecv.at[1], at(dz=8 - q)).wait()

        for d in range(1, 4):
            start(copy(s2r, s3r.at[d - 1], psend.at[2], crecv.at[2], at(dx=d)))

    def chosen3():
        sent(s3r, crecv.at[2])
        total = s2r[...].astype(F32) + jnp.sum(s3r[...].astype(F32), axis=0)
        s3s[...] = total.astype(BF16)
        for d in range(1, 4):
            start(copy(s3s, s4r.at[d - 1], psend.at[3], crecv.at[3], at(dy=d)))

    def chosen4():
        sent(s4r, crecv.at[3])
        total = s3s[...].astype(F32) + jnp.sum(s4r[...].astype(F32), axis=0)
        s5s[...] = total.astype(BF16)
        start(copy(s5s, s5r, psend.at[5], crecv.at[5], at(dk=1)))

    def chosen5():
        sent(s5r, crecv.at[5])
        total = s5s[...].astype(F32) + s5r[...].astype(F32)
        whole = jnp.concatenate([total[:PICKS], total[PICKS:]], axis=1)
        chosen[...] = jnp.concatenate([whole, whole], axis=0).astype(BF16)

    pair = 2 * CAP
    prow, crow = 2 * RING * pair, RING * pair

    def assemble(group):
        def put(dst, row, ref, s):
            a, b = ref[s, PAIRS[group][0]].astype(F32), ref[s, PAIRS[group][1]].astype(F32)
            dst[row : row + pair, :half] = jnp.concatenate([a[:CAP], b[:CAP]], axis=0).astype(BF16)
            dst[row : row + pair, half:] = jnp.concatenate([a[CAP:], b[CAP:]], axis=0).astype(BF16)

        for s in range(RING):
            put(points, group * prow + s * pair, rawx, s)
            put(points, group * prow + crow + s * pair, raws, s)
            put(cands, group * crow + s * pair, *((rawx, 0) if s == 0 else (rawy, s - 1)))

    def cover(group):
        near = rows_dot(points[group * prow : (group + 1) * prow, :], chosen[...]) * scale
        cov[group * prow : (group + 1) * prow, :] = jnp.maximum(jnp.max(near, axis=1, keepdims=True), 0.0)

    def fold():
        terms = jnp.maximum(rows_dot(points[...], cands[...]) * scale - cov[...], 0.0)
        return jnp.sum(terms.reshape(-1, 8, cands.shape[0]), axis=0)

    zs = {}
    zs[1] = zcopy(1)
    zs[2] = zcopy(2)
    sort_waves(0)
    level0(0)
    sort_waves(3, 4)
    zs[3] = zcopy(3)
    zs[4] = zcopy(4)
    sort_picks()
    sort_waves(5, 6)
    zs[5] = zcopy(5)
    zs[6] = zcopy(6)
    sort_waves(7)
    chosen0()
    level0(1)
    level1(0)
    level0(2)
    chosen1()
    zs[7] = zcopy(7)
    level1(1)
    level2(0)
    level0(3)
    chosen2()
    level1(2)
    level2(1)
    level3(0)
    level3(1)
    assemble(0)
    level0(4)
    chosen3()
    level1(3)
    level2(2)
    chosen4()
    level3(2)
    assemble(1)
    level2(3)
    level1(4)
    level2(4)
    chosen5()
    cover(0)
    cover(1)
    level3(3)
    assemble(2)
    cover(2)
    level3(4)
    assemble(3)
    cover(3)
    gains = jnp.sum(fold(), axis=0, keepdims=True)

    for b in range(WIN // 2):
        part = gains[:, b * crow : (b + 1) * crow]
        gs[b] = jnp.concatenate([part, jnp.zeros((1, 256 - crow), F32)], axis=1)
    steps = (0, 1, 3, 2)
    for n in reversed(range(WIN)):
        for i, dy in reversed(list(enumerate(steps))):
            if i == n == 0:
                gz[0] = gs[WIN // 2 - 1]
            else:
                start(copy(gs.at[(n + 7) % 8 // 2], gz.at[i * WIN + n], gsend, grecv, at(dy=dy, dz=WAVES[n])))
    shift = lax.rem(wave + 1, 2) * CAP + place
    spread = jnp.where(lax.broadcasted_iota(I32, (128, rows), 0) == shift, 1.0, 0.0)
    mine = lax.broadcasted_iota(I32, (WIN, rows), 0) == wave
    sent(sort, zsend)
    sent(rawy, xsend)
    sent(rawy, ysend)
    sent(raws, ksend)
    sent(s1r, psend.at[0])
    sent(s3r, psend.at[2])
    sent(s4r, psend.at[3])
    sent(s2x, psend.at[4])
    sent(s5r, psend.at[5])
    sent(gz.at[pl.ds(1, 31)], grecv)
    total = gz[0:WIN].reshape(WIN, 256)
    for i, s in ((1, 2), (2, 1), (3, 3)):
        total = total + pltpu.roll(gz[i * WIN : (i + 1) * WIN].reshape(WIN, 256), 256 - s * pair, 1)
    placed = jnp.dot(total[:, :128], spread, precision=lax.Precision.HIGHEST, preferred_element_type=F32)
    out[...] = jnp.sum(jnp.where(mine, placed, 0.0), axis=0, keepdims=True) * GAIN_SCALE
    sent(gz.at[pl.ds(1, 31)], gsend)


def shards(embeddings, membership, selected):
    rows, width = embeddings.shape
    half = width // 2
    chunk, short = (2 * CAP, half), (2 * PICKS, half)
    dma = pltpu.SemaphoreType.DMA
    gains = pl.pallas_call(
        kernel,
        out_shape=jax.ShapeDtypeStruct((1, rows), F32),
        in_specs=[pl.BlockSpec(memory_space=pltpu.HBM)] * 3,
        out_specs=pl.BlockSpec(memory_space=pltpu.VMEM),
        scratch_shapes=[
            pltpu.VMEM((rows, width), BF16),
            pltpu.VMEM((1, rows), I32),
            pltpu.VMEM(selected.shape, I32),
            pltpu.VMEM((7,) + chunk, BF16),
            pltpu.VMEM((2, 4) + short, BF16),
            pltpu.VMEM((4, 8) + chunk, BF16),
            pltpu.VMEM((3, 8) + chunk, BF16),
            pltpu.VMEM((4, 8) + chunk, BF16),
            pltpu.VMEM((4,) + short, BF16),
            pltpu.VMEM((4,) + short, BF16),
            pltpu.VMEM((3,) + short, BF16),
            pltpu.VMEM(short, BF16),
            pltpu.VMEM(short, BF16),
            pltpu.VMEM((3,) + short, BF16),
            pltpu.VMEM(short, BF16),
            pltpu.VMEM((3,) + short, BF16),
            pltpu.VMEM(short, BF16),
            pltpu.VMEM(short, BF16),
            pltpu.VMEM((2 * PICKS, width), BF16),
            pltpu.VMEM((8 * 8 * CAP, width), BF16),
            pltpu.VMEM((8 * 4 * CAP, width), BF16),
            pltpu.VMEM((8 * 8 * CAP, 1), F32),
            pltpu.VMEM((4, 1, 256), F32),
            pltpu.VMEM((32, 1, 256), F32),
            dma((3,)), dma, dma, dma, dma, dma((6,)), dma((8, 8)), dma((6,)), dma, dma,
        ],
        compiler_params=pltpu.CompilerParams(
            collective_id=0, has_side_effects=True, vmem_limit_bytes=62 * 1024 * 1024
        ),
    )(embeddings, membership.reshape(1, rows), selected)
    return gains.reshape(rows)


def solution(mesh):
    in_specs = (P(("row", "col"), None), P(("row", "col"), None), P())
    out_specs = P(("row", "col"))
    return jax.shard_map(shards, mesh=mesh, in_specs=in_specs, out_specs=out_specs, check_vma=False)
```
